32 devices in a mesh: frame: 16 (over z, x, core), clip: 2 (over y).
Axes of the slice: x: 2, y: 2, z: 4, core: 2. Of those that a mesh axis runs over, the one named last changes fastest.
Arguments:
- latents: bfloat16 [64, 576, 640], P(('clip', 'frame')), parts along dimension 0, may hold values from -6 to 6
- offsets: int32 [32], P(('clip', 'frame')), parts along dimension 0, may hold values from 0 to 1
- source_device: int32 [2], P('clip'), parts along dimension 0, may hold values from 0 to 15
- reference_bank: bfloat16 [32, 576, 640], P(('clip', 'frame')), parts along dimension 0, may hold values from -6 to 6
- spatial_in: bfloat16 [640, 960], P('frame'), may hold values from -7.1151247 to 7.1151247
- spatial_out: bfloat16 [320, 640], P(None, 'frame'), may hold values from -0.3125 to 0.3125
- temporal_in: bfloat16 [640, 960], P('frame'), may hold values from -7.1151247 to 7.1151247
- temporal_out: bfloat16 [320, 640], P(None, 'frame'), may hold values from -0.3125 to 0.3125
Outputs:
- blended: bfloat16 [64, 576, 640], P(('clip', 'frame')), parts along dimension 0
The draws below stay inside these ranges and needn't reach their ends.
There are 2 independent parts, one for each index of `clip`. The reference program is written for one: setup_inputs(seed, part) draws one part's arguments, and reference() takes and returns one part's arrays. A program takes and returns all parts, laid end to end along the dimension named above; an argument that names none is the same for every part. Nothing has to cross between parts.
All inputs are finite; a program needn't handle non-finite values.
Results may differ from the reference program's by a relative error of at most 0.018.
The reference program's roundings to bfloat16 on the way count: a program that leaves them out, or rounds other values in their place, can miss the bound.
Values may be sent and summed in bfloat16 or wider, within the bound.
A program may use at most 128 MiB of HBM per device.

```python
import jax
import jax.numpy as jnp
from jax import lax

C = 640
HW = 576
HEADS = 4
HEAD_DIM = 80
WIN = 16
FR_DEV = 2
INNER = 320
FRAMES = 32
N_FRAME = 16


def projection_base(key):
    inner = HEADS * HEAD_DIM
    values = jnp.clip(jax.random.normal(key, (C, 3 * inner), jnp.float32), -6.0, 6.0)
    return values * C ** (-0.5)


def draw_spatial_in(key, part):
    values = projection_base(jax.random.fold_in(key, 11))
    return values.astype(jnp.bfloat16)


def draw_temporal_in(key, part):
    values = projection_base(jax.random.fold_in(key, 23))
    return values.astype(jnp.bfloat16)


def touch_ends(array, rng, low, top_value):
    longest = array.shape.index(max(array.shape))
    spots = []
    for shift in (0, 1):
        where = [jax.random.randint(jax.random.fold_in(rng, axis), (), 0, length) for axis, length in enumerate(array.shape)]
        where[longest] = (where[longest] + shift) % array.shape[longest]
        spots.append(tuple(where))
    return array.at[spots[0]].set(low).at[spots[1]].set(top_value)


def steps_of(key, dims, cuts, least, high):
    factor_of, own = 1.0, jax.random.fold_in(key, 6)
    for axis_at, blocks in cuts:
        heights = jnp.exp(jax.random.uniform(jax.random.fold_in(own, axis_at), (blocks,), jnp.float32, least / len(cuts), high / len(cuts)))
        factor_of = factor_of * jnp.repeat(heights, dims[axis_at] // blocks).reshape([-1 if axis == axis_at else 1 for axis in range(len(dims))])
    return factor_of


def noise(key, shape, deviation, reach, split=(), kind=jnp.bfloat16):
    values = deviation * jax.random.normal(key, shape, jnp.float32)
    if split:
        values = values * steps_of(key, shape, split, -0.22, 0.18)
    return jnp.clip(values, -reach, reach).astype(kind)


def setup_inputs(seed: int = 0, part: int = 0) -> dict:
    key_of = jax.random.split(jax.random.key(seed), 9)
    own_keys = jax.random.split(jax.random.fold_in(key_of[8], part), 9)
    return {
        "latents": noise(own_keys[0], (FRAMES, HW, C), 1.0, 6.0, ((0, 16),)),
        "offsets": touch_ends(jax.random.randint(own_keys[1], (N_FRAME,), 0, 2), jax.random.fold_in(own_keys[1], 1), 0, 1).astype(jnp.int32),
        "source_device": jax.random.randint(own_keys[2], (1,), 0, N_FRAME).astype(jnp.int32),
        "reference_bank": noise(own_keys[3], (N_FRAME, HW, C), 1.0, 6.0, ((0, 16),)),
        "spatial_in": draw_spatial_in(jax.random.fold_in(key_of[8], 71), part),
        "spatial_out": noise(key_of[5], (INNER, C), INNER ** -0.5, 0.3125, ((1, 16),)),
        "temporal_in": draw_temporal_in(jax.random.fold_in(key_of[8], 71), part),
        "temporal_out": noise(key_of[7], (INNER, C), INNER ** -0.5, 0.3125, ((1, 16),)),
    }


def normalize(values):
    values = values.astype(jnp.float32)
    center = values - lax.optimization_barrier(jnp.mean(values, axis=-1, keepdims=True))
    spread = lax.optimization_barrier(jnp.mean(center * center, axis=-1, keepdims=True))
    return center * lax.rsqrt(spread + 1e-05)

def attend(queries, keys, values):
    count = queries.shape[0]
    scale = HEAD_DIM ** (-0.5)
    qf = queries.astype(jnp.float32).reshape(count, HEADS, HEAD_DIM)
    kf = keys.astype(jnp.float32).reshape(keys.shape[0], HEADS, HEAD_DIM)
    vf = values.astype(jnp.float32).reshape(values.shape[0], HEADS, HEAD_DIM)
    scores = jnp.einsum('qhd,khd->hqk', qf, kf) * scale
    scores = scores - lax.optimization_barrier(jnp.max(scores, axis=-1, keepdims=True))
    expo = jnp.exp(scores)
    weights = (expo / lax.optimization_barrier(jnp.sum(expo, axis=-1, keepdims=True))).astype(jnp.bfloat16)
    result = jnp.einsum('hqk,khd->qhd', weights.astype(jnp.float32), vf)
    return result.reshape(count, HEADS * HEAD_DIM).astype(jnp.bfloat16)

def reference(latents, offsets, source_device, reference_bank, spatial_in, spatial_out, temporal_in, temporal_out):
    inner = HEADS * HEAD_DIM
    frames_total = latents.shape[0]
    hidden = normalize(latents).astype(jnp.bfloat16)
    picked = lax.dynamic_index_in_dim(reference_bank, source_device[0], 0, keepdims=False)
    ref_hidden = normalize(picked).astype(jnp.bfloat16)
    ref_kv = jnp.dot(ref_hidden, spatial_in[:, inner:], preferred_element_type=jnp.float32).astype(jnp.bfloat16)
    proj = jnp.dot(hidden.reshape(-1, C), spatial_in, preferred_element_type=jnp.float32).astype(jnp.bfloat16)
    proj = proj.reshape(frames_total, HW, 3 * inner)

    def spatial_frame(block):
        keys = jnp.concatenate([block[:, inner:2 * inner], ref_kv[:, :inner]], axis=0)
        vals = jnp.concatenate([block[:, 2 * inner:], ref_kv[:, inner:]], axis=0)
        return attend(block[:, :inner], keys, vals)
    attended = lax.map(spatial_frame, proj)
    mixed = jnp.dot(attended.reshape(-1, inner), spatial_out, preferred_element_type=jnp.float32)
    first = (latents.astype(jnp.float32).reshape(-1, C) + mixed).astype(jnp.bfloat16)
    hidden_two = normalize(first).astype(jnp.bfloat16)
    tproj = jnp.dot(hidden_two, temporal_in, preferred_element_type=jnp.float32).astype(jnp.bfloat16)
    tproj = tproj.reshape(frames_total, HW, 3, HEADS, HEAD_DIM).transpose(2, 3, 1, 0, 4)
    times = jnp.arange(frames_total, dtype=jnp.int32)
    shard = times // FR_DEV
    starts = shard * FR_DEV - (WIN // 2 - 1) + jnp.take(offsets, shard)
    valid = (times[None, :] >= starts[:, None]) & (times[None, :] < starts[:, None] + WIN)
    scale = HEAD_DIM ** (-0.5)

    def temporal_head(triple):
        qh, kh, vh = triple
        scores = jnp.einsum('tfd,tud->tfu', qh.astype(jnp.float32), kh.astype(jnp.float32)) * scale
        scores = jnp.where(valid[None], scores, -1e+30)
        scores = scores - lax.optimization_barrier(jnp.max(scores, axis=-1, keepdims=True))
        expo = jnp.exp(scores)
        weights = (expo / lax.optimization_barrier(jnp.sum(expo, axis=-1, keepdims=True))).astype(jnp.bfloat16)
        return jnp.einsum('tfu,tud->tfd', weights.astype(jnp.float32), vh.astype(jnp.float32))
    heads_out = lax.map(temporal_head, (tproj[0], tproj[1], tproj[2]))
    tattended = heads_out.transpose(2, 1, 0, 3).reshape(frames_total * HW, inner).astype(jnp.bfloat16)
    second = jnp.dot(tattended, temporal_out, preferred_element_type=jnp.float32)
    blended = (first.astype(jnp.float32) + second).astype(jnp.bfloat16)
    return blended.reshape(frames_total, HW, C)
```

```python
import functools
import math

import jax
import jax.numpy as jnp
from jax import lax
from jax.experimental import pallas as pl
from jax.experimental.pallas import tpu as pltpu
from jax.sharding import PartitionSpec as P

C = 640
HW = 576
HEADS = 4
HEAD_DIM = 80
INNER = 320
WIDE = 384
WIN = 16
MESH = pl.DeviceIdType.MESH
FACTOR = HEAD_DIM ** (-0.5) * math.log2(math.e)
VMEM_LIMIT = 60 * 1024 * 1024
SPANS = tuple(
    (h * HEAD_DIM // 128, (h * HEAD_DIM + HEAD_DIM - 1) // 128 + 1) for h in range(HEADS)
)


def up16(count):
    return -(-count // 16) * 16


def normalize(values):
    values = values.astype(jnp.float32)
    center = values - jnp.mean(values, axis=-1, keepdims=True)
    spread = jnp.mean(center * center, axis=-1, keepdims=True)
    return center * lax.rsqrt(spread + 1e-05)


def dot(a, b):
    return jnp.dot(a, b, preferred_element_type=jnp.float32)


def dot_t(a, b):
    return lax.dot_general(a, b, (((1,), (1,)), ((), ())), preferred_element_type=jnp.float32)


def remote(src, dst, send, recv, peer):
    return pltpu.make_async_remote_copy(
        src_ref=src, dst_ref=dst, send_sem=send, recv_sem=recv,
        device_id={"frame": peer}, device_id_type=MESH,
    )


def greet(n, me):
    barrier = pltpu.get_barrier_semaphore()
    for k in range(1, n):
        pl.semaphore_signal(
            barrier, inc=1, device_id={"frame": lax.rem(me + k, n)}, device_id_type=MESH
        )
    pl.semaphore_wait(barrier, n - 1)


def exchange_kernel(n, x_ref, o_ref, send, recv, local):
    me = lax.axis_index("frame")
    greet(n, me)
    copies = []
    for k in range(1, n):
        peer = lax.rem(me + k, n)
        copy = remote(x_ref.at[peer], o_ref.at[me], send.at[k], recv.at[k], peer)
        copy.start()
        copies.append(copy)
    own = pltpu.make_async_copy(x_ref.at[me], o_ref.at[me], local)
    own.start()
    own.wait()
    for copy in copies:
        copy.wait()


def exchange(x, ident):
    n = x.shape[0]
    return pl.pallas_call(
        functools.partial(exchange_kernel, n),
        out_shape=jax.ShapeDtypeStruct(x.shape, x.dtype),
        in_specs=[pl.BlockSpec(memory_space=pl.ANY)],
        out_specs=pl.BlockSpec(memory_space=pl.ANY),
        scratch_shapes=[
            pltpu.SemaphoreType.DMA((n,)),
            pltpu.SemaphoreType.DMA((n,)),
            pltpu.SemaphoreType.DMA,
        ],
        compiler_params=pltpu.CompilerParams(collective_id=ident, has_side_effects=True),
    )(x)


def collect_kernel(
    n, rows, holders, src_ref, bank_ref, w_ref, ref_ref, wall_ref,
    got, chunk, bsend, brecv, wsend, wrecv, rsend, rrecv, local,
):
    me = lax.axis_index("frame")
    sub, level = lax.rem(me, 4), me // 4
    levels = n // 4
    xmate = level * 4 + lax.rem(sub + 2, 4)
    cmate = me + 1 - 2 * lax.rem(me, 2)
    greet(n, me)
    for k in range(1, n):
        peer = lax.rem(me + k, n)

        @pl.when(peer < holders)
        def _():
            start = pl.multiple_of(peer * rows, 16)
            remote(
                bank_ref.at[0, pl.ds(start, rows)], got.at[me], bsend.at[k], brecv.at[k], peer
            ).start()

    @pl.when(me < holders)
    def _():
        start = pl.multiple_of(me * rows, 16)
        own = pltpu.make_async_copy(bank_ref.at[0, pl.ds(start, rows)], got.at[me], local.at[0])
        own.start()
        own.wait()

    place = pltpu.make_async_copy(w_ref, wall_ref.at[me], local.at[1])
    place.start()

    def z_copy(k):
        peer = lax.rem(me + 4 * k, n)
        return remote(w_ref, wall_ref.at[me], wsend.at[0, k], wrecv.at[0, k], peer)

    def hop_copy(stage, block, slot, peer):
        part = wall_ref.at[block]
        return remote(part, part, wsend.at[stage, slot], wrecv.at[stage, slot], peer)

    for k in range(1, levels):
        z_copy(k).start()
    place.wait()
    firsts = []
    for k in range(levels):
        block = lax.rem(me + n - 4 * k, n)
        if k:
            z_copy(k).wait_recv()
        copy = hop_copy(1, block, k, xmate)
        copy.start()
        firsts.append(copy)
        last = hop_copy(2, block, k, cmate)
        last.start()
        firsts.append(last)
    for k in range(1, n):
        peer = lax.rem(me + k, n)

        @pl.when(me < holders)
        def _():
            start = pl.multiple_of(me * rows, 16)
            remote(
                bank_ref.at[0, pl.ds(start, rows)], got.at[me], bsend.at[k], brecv.at[k], peer
            ).wait_recv()

        @pl.when(peer < holders)
        def _():
            start = pl.multiple_of(peer * rows, 16)
            remote(
                bank_ref.at[0, pl.ds(start, rows)], got.at[me], bsend.at[k], brecv.at[k], peer
            ).wait_send()

    @pl.when(me < holders)
    def _():
        chunk[...] = got[src_ref[0]]
        for k in range(1, n):
            peer = lax.rem(me + k, n)
            remote(chunk, ref_ref.at[me], rsend.at[k], rrecv.at[k], peer).start()
        own = pltpu.make_async_copy(chunk, ref_ref.at[me], local.at[0])
        own.start()
        own.wait()

    for k in range(levels):
        block = lax.rem(xmate + n - 4 * k, n)
        hop_copy(1, block, k, xmate).wait_recv()
        last = hop_copy(2, block, levels + k, cmate)
        last.start()
        firsts.append(last)
    for k in range(levels):
        for side in range(2):
            origin = cmate if side == 0 else lax.rem(cmate // 4 * 4 + lax.rem(cmate + 2, 4), n)
            block = lax.rem(origin + n - 4 * k, n)
            hop_copy(2, block, side * levels + k, cmate).wait_recv()
    for copy in firsts:
        copy.wait_send()
    for k in range(1, levels):
        z_copy(k).wait_send()
    for k in range(1, n):
        peer = lax.rem(me + k, n)
        sender = lax.rem(me + n - k, n)

        @pl.when(sender < holders)
        def _():
            remote(chunk, ref_ref.at[sender], rsend.at[k], rrecv.at[k], peer).wait_recv()

        @pl.when(me < holders)
        def _():
            remote(chunk, ref_ref.at[me], rsend.at[k], rrecv.at[k], peer).wait_send()


def collect(source, bank, weights, n, ident):
    rows = up16(-(-HW // n))
    holders = HW // rows
    any_spec = pl.BlockSpec(memory_space=pl.ANY)
    dma = pltpu.SemaphoreType.DMA
    return pl.pallas_call(
        functools.partial(collect_kernel, n, rows, holders),
        out_shape=(
            jax.ShapeDtypeStruct((holders, rows, C), jnp.bfloat16),
            jax.ShapeDtypeStruct((n,) + weights.shape, jnp.bfloat16),
        ),
        in_specs=[pl.BlockSpec(memory_space=pltpu.SMEM), any_spec, any_spec],
        out_specs=(any_spec, any_spec),
        scratch_shapes=[
            pltpu.VMEM((n, rows, C), jnp.bfloat16),
            pltpu.VMEM((rows, C), jnp.bfloat16),
            dma((n,)), dma((n,)),
            dma((3, n)), dma((3, n)),
            dma((n,)), dma((n,)),
            dma((2,)),
        ],
        compiler_params=pltpu.CompilerParams(collective_id=ident, has_side_effects=True),
    )(source, bank, weights)


def heads_of(queries, keys, values, bias):
    lane = lax.broadcasted_iota(jnp.int32, (1, WIDE), 1)
    blocks = [None] * (WIDE // 128)
    for head, (low, high) in enumerate(SPANS):
        inside = (lane >= head * HEAD_DIM) & (lane < (head + 1) * HEAD_DIM)
        inside = inside[:, low * 128 : high * 128]
        q = queries(low, high)
        q = jnp.where(inside, q, jnp.zeros_like(q))
        raw = dot_t(q, keys(low, high))
        if bias is not None:
            raw = raw + bias
        expo = jnp.exp2((raw - jnp.max(raw, axis=-1, keepdims=True)) * FACTOR)
        total = jnp.sum(expo, axis=-1, keepdims=True)
        weights = (expo * (1.0 / total)).astype(jnp.bfloat16)
        part = jnp.where(inside, dot(weights, values(low, high)), 0.0)
        for b in range(low, high):
            piece = part[:, (b - low) * 128 : (b - low + 1) * 128]
            blocks[b] = piece if blocks[b] is None else blocks[b] + piece
    return jnp.concatenate(blocks, axis=1).astype(jnp.bfloat16)


def spatial_kernel(step, lat_ref, w_ref, picked_ref, first_ref, hid_ref, qs, ks, vs):
    @pl.when(pl.program_id(0) == 0)
    def _():
        hidden = normalize(picked_ref[...]).astype(jnp.bfloat16)
        ks[HW:, :] = dot(hidden, w_ref[:, WIDE : 2 * WIDE]).astype(jnp.bfloat16)
        vs[HW:, :] = dot(hidden, w_ref[:, 2 * WIDE : 3 * WIDE]).astype(jnp.bfloat16)

    hidden = normalize(lat_ref[0]).astype(jnp.bfloat16)
    qs[...] = dot(hidden, w_ref[:, :WIDE]).astype(jnp.bfloat16)
    ks[:HW, :] = dot(hidden, w_ref[:, WIDE : 2 * WIDE]).astype(jnp.bfloat16)
    vs[:HW, :] = dot(hidden, w_ref[:, 2 * WIDE : 3 * WIDE]).astype(jnp.bfloat16)

    def rows_of(at, carry):
        rows = pl.ds(pl.multiple_of(at * step, step), step)
        attended = heads_of(
            lambda a, b: qs[rows, a * 128 : b * 128],
            lambda a, b: ks[:, a * 128 : b * 128],
            lambda a, b: vs[:, a * 128 : b * 128],
            None,
        )
        mixed = dot_t(attended, w_ref[:, 3 * WIDE :])
        first = (lat_ref[0, rows, :].astype(jnp.float32) + mixed).astype(jnp.bfloat16)
        first_ref[0, rows, :] = first
        hid_ref[0, rows, :] = normalize(first).astype(jnp.bfloat16)
        return carry

    lax.fori_loop(0, HW // step, rows_of, 0)


def spatial(latents, weights, picked):
    frames = latents.shape[0]
    block = pl.BlockSpec((1, HW, C), lambda f: (f, 0, 0))
    shape = jax.ShapeDtypeStruct(latents.shape, jnp.bfloat16)
    return pl.pallas_call(
        functools.partial(spatial_kernel, 192),
        grid=(frames,),
        out_shape=(shape, shape),
        in_specs=[
            block,
            pl.BlockSpec((C, 4 * WIDE), lambda f: (0, 0)),
            pl.BlockSpec((HW, C), lambda f: (0, 0)),
        ],
        out_specs=(block, block),
        scratch_shapes=[
            pltpu.VMEM((HW, WIDE), jnp.bfloat16),
            pltpu.VMEM((2 * HW, WIDE), jnp.bfloat16),
            pltpu.VMEM((2 * HW, WIDE), jnp.bfloat16),
        ],
        cost_estimate=pl.CostEstimate(
            flops=9_000_000_000, bytes_accessed=9_000_000, transcendentals=5_400_000
        ),
        compiler_params=pltpu.CompilerParams(vmem_limit_bytes=VMEM_LIMIT),
    )(latents, weights, picked)


def temporal_kernel(group, x_ref, w_ref, bias_ref, out_ref, proj):
    proj[...] = dot(x_ref[...], w_ref[:, : 3 * WIDE]).astype(jnp.bfloat16)
    bias = bias_ref[...]
    for at in range(x_ref.shape[0] // group):
        rows = slice(at * group, (at + 1) * group)
        attended = heads_of(
            lambda a, b: proj[rows, a * 128 : b * 128],
            lambda a, b: proj[rows, WIDE + a * 128 : WIDE + b * 128],
            lambda a, b: proj[rows, 2 * WIDE + a * 128 : 2 * WIDE + b * 128],
            bias,
        )
        out_ref[rows, :] = attended[:, :INNER]


def temporal(x, weights, bias):
    rows = x.shape[0]
    return pl.pallas_call(
        functools.partial(temporal_kernel, bias.shape[0]),
        out_shape=jax.ShapeDtypeStruct((rows, INNER), jnp.bfloat16),
        in_specs=[pl.BlockSpec(memory_space=pltpu.VMEM)] * 3,
        out_specs=pl.BlockSpec(memory_space=pltpu.VMEM),
        scratch_shapes=[pltpu.VMEM((rows, 3 * WIDE), jnp.bfloat16)],
        compiler_params=pltpu.CompilerParams(vmem_limit_bytes=VMEM_LIMIT),
    )(x, weights, bias)


def widen(weights):
    parts = weights.reshape(weights.shape[0], 4, INNER)
    parts = jnp.pad(parts, ((0, 0), (0, 0), (0, WIDE - INNER)))
    return parts.reshape(weights.shape[0], 4 * WIDE)


def body(
    latents, offsets, source_device, reference_bank,
    spatial_in, spatial_out, temporal_in, temporal_out,
):
    n = lax.axis_size("frame")
    frames = latents.shape[0]
    total = n * frames
    spots = HW // n
    depth = spatial_in.shape[0]

    packed_t = jnp.concatenate([temporal_in, temporal_out.T], axis=1)
    gathered_t = lax.all_gather(packed_t, "frame", axis=0, tiled=True)
    starts = lax.all_gather(offsets, "frame", axis=0, tiled=True)

    packed_s = jnp.concatenate([spatial_in, spatial_out.T], axis=1)
    packed_s = jnp.pad(packed_s, ((0, up16(depth) - depth), (0, 0)))
    picked, gathered_s = collect(source_device, reference_bank, packed_s, n, 0)
    weights_s = widen(gathered_s[:, :depth].reshape(C, 4 * INNER))
    first, hidden = spatial(latents, weights_s, picked.reshape(HW, C))

    held = up16(frames * spots)
    x = hidden.reshape(frames, n, spots, C).transpose(1, 0, 2, 3).reshape(n, frames * spots, C)
    x = jnp.pad(x, ((0, 0), (0, held - frames * spots), (0, 0)))
    x = exchange(x, 1)[:, : frames * spots]
    x = x.reshape(total, spots, C).transpose(1, 0, 2).reshape(spots * total, C)

    group = max(128, total)
    row = jnp.arange(group, dtype=jnp.int32)
    time, spot = row % total, row // total
    begin = (time // frames) * frames - (WIN // 2 - 1) + jnp.repeat(
        jnp.tile(starts, group // total), frames
    )
    valid = (
        (spot[:, None] == spot[None, :])
        & (time[None, :] >= begin[:, None])
        & (time[None, :] < begin[:, None] + WIN)
    )
    bias = jnp.where(valid, 0.0, -1e30).astype(jnp.float32)
    back = temporal(x, widen(gathered_t), bias)

    back = back.reshape(spots, n, frames, INNER).transpose(1, 2, 0, 3)
    back = back.reshape(n, frames * spots, INNER)
    back = jnp.pad(back, ((0, 0), (0, held - frames * spots), (0, 0)))
    back = exchange(back, 2)[:, : frames * spots]
    back = back.reshape(n, frames, spots, INNER).transpose(1, 0, 2, 3).reshape(frames * HW, INNER)
    second = dot_t(back, gathered_t[:, 3 * INNER :])
    blended = (first.astype(jnp.float32).reshape(frames * HW, C) + second).astype(jnp.bfloat16)
    return blended.reshape(frames, HW, C)


def solution(mesh):
    placed = (
        P(("clip", "frame"), None, None),
        P(("clip", "frame")),
        P("clip"),
        P(("clip", "frame"), None, None),
        P("frame", None),
        P(None, "frame"),
        P("frame", None),
        P(None, "frame"),
    )
    return jax.shard_map(
        body, mesh=mesh, in_specs=placed,
        out_specs=P(("clip", "frame"), None, None), check_vma=False,
    )
```

```python
import functools
import math

import jax
import jax.numpy as jnp
from jax import lax
from jax.experimental import pallas as pl
from jax.experimental.pallas import tpu as pltpu
from jax.sharding import PartitionSpec as P

C = 640
HW = 576
HEADS = 4
HEAD_DIM = 80
INNER = 320
WIDE = 384
WIN = 16
PLANE = 4
CLUSTER = 16
PIECES = 3
MESH = pl.DeviceIdType.MESH
FACTOR = HEAD_DIM ** (-0.5) * math.log2(math.e)
VMEM_LIMIT = 60 * 1024 * 1024
SPANS = tuple(
    (h * HEAD_DIM // 128, (h * HEAD_DIM + HEAD_DIM - 1) // 128 + 1) for h in range(HEADS)
)


def up16(count):
    return -(-count // 16) * 16


def normalize(values):
    values = values.astype(jnp.float32)
    center = values - jnp.mean(values, axis=-1, keepdims=True)
    spread = jnp.mean(center * center, axis=-1, keepdims=True)
    return center * lax.rsqrt(spread + 1e-05)


def dot(a, b):
    return jnp.dot(a, b, preferred_element_type=jnp.float32)


def dot_t(a, b):
    return lax.dot_general(a, b, (((1,), (1,)), ((), ())), preferred_element_type=jnp.float32)


def remote(src, dst, send, recv, peer):
    return pltpu.make_async_remote_copy(
        src_ref=src, dst_ref=dst, send_sem=send, recv_sem=recv,
        device_id={"frame": peer}, device_id_type=MESH,
    )


def greet(n, me):
    barrier = pltpu.get_barrier_semaphore()
    for k in range(1, n):
        pl.semaphore_signal(
            barrier, inc=1, device_id={"frame": lax.rem(me + k, n)}, device_id_type=MESH
        )
    pl.semaphore_wait(barrier, n - 1)


def collect_kernel(
    n, rows, holders, src_ref, bank_ref, w_ref, ref_ref, wall_ref,
    got, chunk, bsend, brecv, wsend, wrecv, rsend, rrecv, local,
):
    me = lax.axis_index("frame")
    sub, level = lax.rem(me, 4), me // 4
    levels = n // 4
    xmate = level * 4 + lax.rem(sub + 2, 4)
    cmate = me + 1 - 2 * lax.rem(me, 2)
    greet(n, me)
    for k in range(1, n):
        peer = lax.rem(me + k, n)

        @pl.when(peer < holders)
        def _():
            start = pl.multiple_of(peer * rows, 16)
            remote(
                bank_ref.at[0, pl.ds(start, rows)], got.at[me], bsend.at[k], brecv.at[k], peer
            ).start()

    @pl.when(me < holders)
    def _():
        start = pl.multiple_of(me * rows, 16)
        own = pltpu.make_async_copy(bank_ref.at[0, pl.ds(start, rows)], got.at[me], local.at[0])
        own.start()
        own.wait()

    place = pltpu.make_async_copy(w_ref, wall_ref.at[me], local.at[1])
    place.start()

    def z_copy(k):
        peer = lax.rem(me + 4 * k, n)
        return remote(w_ref, wall_ref.at[me], wsend.at[0, k], wrecv.at[0, k], peer)

    def hop_copy(stage, block, slot, peer):
        part = wall_ref.at[block]
        return remote(part, part, wsend.at[stage, slot], wrecv.at[stage, slot], peer)

    for k in range(1, levels):
        z_copy(k).start()
    place.wait()
    firsts = []
    for k in range(levels):
        block = lax.rem(me + n - 4 * k, n)
        if k:
            z_copy(k).wait_recv()
        copy = hop_copy(1, block, k, xmate)
        copy.start()
        firsts.append(copy)
        last = hop_copy(2, block, k, cmate)
        last.start()
        firsts.append(last)
    for k in range(1, n):
        peer = lax.rem(me + k, n)

        @pl.when(me < holders)
        def _():
            start = pl.multiple_of(me * rows, 16)
            remote(
                bank_ref.at[0, pl.ds(start, rows)], got.at[me], bsend.at[k], brecv.at[k], peer
            ).wait_recv()

        @pl.when(peer < holders)
        def _():
            start = pl.multiple_of(peer * rows, 16)
            remote(
                bank_ref.at[0, pl.ds(start, rows)], got.at[me], bsend.at[k], brecv.at[k], peer
            ).wait_send()

    @pl.when(me < holders)
    def _():
        chunk[...] = got[src_ref[0]]
        for k in range(1, n):
            peer = lax.rem(me + k, n)
            remote(chunk, ref_ref.at[me], rsend.at[k], rrecv.at[k], peer).start()
        own = pltpu.make_async_copy(chunk, ref_ref.at[me], local.at[0])
        own.start()
        own.wait()

    for k in range(levels):
        block = lax.rem(xmate + n - 4 * k, n)
        hop_copy(1, block, k, xmate).wait_recv()
        last = hop_copy(2, block, levels + k, cmate)
        last.start()
        firsts.append(last)
    for k in range(levels):
        for side in range(2):
            origin = cmate if side == 0 else lax.rem(cmate // 4 * 4 + lax.rem(cmate + 2, 4), n)
            block = lax.rem(origin + n - 4 * k, n)
            hop_copy(2, block, side * levels + k, cmate).wait_recv()
    for copy in firsts:
        copy.wait_send()
    for k in range(1, levels):
        z_copy(k).wait_send()
    for k in range(1, n):
        peer = lax.rem(me + k, n)
        sender = lax.rem(me + n - k, n)

        @pl.when(sender < holders)
        def _():
            remote(chunk, ref_ref.at[sender], rsend.at[k], rrecv.at[k], peer).wait_recv()

        @pl.when(me < holders)
        def _():
            remote(chunk, ref_ref.at[me], rsend.at[k], rrecv.at[k], peer).wait_send()


def collect(source, bank, weights, n, ident):
    rows = up16(-(-HW // n))
    holders = HW // rows
    any_spec = pl.BlockSpec(memory_space=pl.ANY)
    dma = pltpu.SemaphoreType.DMA
    return pl.pallas_call(
        functools.partial(collect_kernel, n, rows, holders),
        out_shape=(
            jax.ShapeDtypeStruct((holders, rows, C), jnp.bfloat16),
            jax.ShapeDtypeStruct((n,) + weights.shape, jnp.bfloat16),
        ),
        in_specs=[pl.BlockSpec(memory_space=pltpu.SMEM), any_spec, any_spec],
        out_specs=(any_spec, any_spec),
        scratch_shapes=[
            pltpu.VMEM((n, rows, C), jnp.bfloat16),
            pltpu.VMEM((rows, C), jnp.bfloat16),
            dma((n,)), dma((n,)),
            dma((3, n)), dma((3, n)),
            dma((n,)), dma((n,)),
            dma((2,)),
        ],
        compiler_params=pltpu.CompilerParams(collective_id=ident, has_side_effects=True),
    )(source, bank, weights)


def heads_of(queries, keys, values, bias):
    lane = lax.broadcasted_iota(jnp.int32, (1, WIDE), 1)
    blocks = [None] * (WIDE // 128)
    for head, (low, high) in enumerate(SPANS):
        inside = (lane >= head * HEAD_DIM) & (lane < (head + 1) * HEAD_DIM)
        inside = inside[:, low * 128 : high * 128]
        q = queries(low, high)
        q = jnp.where(inside, q, jnp.zeros_like(q))
        raw = dot_t(q, keys(low, high))
        if bias is not None:
            raw = raw + bias
        expo = jnp.exp2((raw - jnp.max(raw, axis=-1, keepdims=True)) * FACTOR)
        total = jnp.sum(expo, axis=-1, keepdims=True)
        weights = (expo * (1.0 / total)).astype(jnp.bfloat16)
        part = jnp.where(inside, dot(weights, values(low, high)), 0.0)
        for b in range(low, high):
            piece = part[:, (b - low) * 128 : (b - low + 1) * 128]
            blocks[b] = piece if blocks[b] is None else blocks[b] + piece
    return jnp.concatenate(blocks, axis=1).astype(jnp.bfloat16)


def block_kernel(
    n, lat_ref, ws_ref, picked_ref, wt_ref, off_ref, out_ref,
    qs, ks, vs, firsts, outgoing, hall, tproj, bias, tatt, back,
    psend, precv, zsend, zrecv, bsend, brecv,
):
    me = lax.axis_index("frame")
    levels = n // PLANE
    level, sub = me // PLANE, lax.rem(me, PLANE)
    base = level * PLANE
    frames = lat_ref.shape[0]
    spots = HW // PLANE
    barrier = pltpu.get_barrier_semaphore()
    has_down, has_up = level > 0, level < levels - 1

    def signal(peer):
        pl.semaphore_signal(barrier, inc=1, device_id={"frame": peer}, device_id_type=MESH)

    def mate(k):
        return base + lax.rem(sub + 1 + k, PLANE)

    for k in range(PLANE - 1):
        signal(mate(k))

    @pl.when(has_up)
    def _():
        signal(me + PLANE)

    @pl.when(has_down)
    def _():
        signal(me - PLANE)

    pl.semaphore_wait(
        barrier, PLANE - 1 + has_up.astype(jnp.int32) + has_down.astype(jnp.int32)
    )

    @pl.when(level == 0)
    def _():
        hall[0] = jnp.zeros(hall.shape[1:], jnp.bfloat16)

    @pl.when(level == levels - 1)
    def _():
        hall[2] = jnp.zeros(hall.shape[1:], jnp.bfloat16)

    def send_plane(f, k):
        return remote(
            outgoing.at[f, k], hall.at[1, frames * sub + f],
            psend.at[f, k], precv.at[f, k], base + lax.rem(sub + 1 + k, PLANE),
        )

    def arrived(f, k):
        source = lax.rem(sub + 2 * PLANE - 1 - k, PLANE)
        return frames * source + f

    def send_level(f, k, up):
        at = arrived(f, k)
        side = 0 if up else 1
        return remote(
            hall.at[1, at], hall.at[0 if up else 2, at],
            zsend.at[side, f, k], zrecv.at[side, f, k], me + PLANE if up else me - PLANE,
        )

    def pass_on(f, k):
        @pl.when(has_up)
        def _():
            send_level(f, k, True).start()

        @pl.when(has_down)
        def _():
            send_level(f, k, False).start()

    hidden = normalize(picked_ref[...]).astype(jnp.bfloat16)
    ks[HW:, :] = dot(hidden, ws_ref[:, WIDE : 2 * WIDE]).astype(jnp.bfloat16)
    vs[HW:, :] = dot(hidden, ws_ref[:, 2 * WIDE : 3 * WIDE]).astype(jnp.bfloat16)
    last = PLANE - 1

    def step(t, carry):
        f, k = t // PLANE, lax.rem(t, PLANE)

        @pl.when(k == 0)
        def _():
            hidden = normalize(lat_ref[f]).astype(jnp.bfloat16)
            qs[...] = dot(hidden, ws_ref[:, :WIDE]).astype(jnp.bfloat16)
            ks[:HW, :] = dot(hidden, ws_ref[:, WIDE : 2 * WIDE]).astype(jnp.bfloat16)
            vs[:HW, :] = dot(hidden, ws_ref[:, 2 * WIDE : 3 * WIDE]).astype(jnp.bfloat16)

        to = lax.rem(sub + 1 + k, PLANE)
        rows = pl.ds(pl.multiple_of(to * spots, 16), spots)
        attended = heads_of(
            lambda a, b: qs[rows, a * 128 : b * 128],
            lambda a, b: ks[:, a * 128 : b * 128],
            lambda a, b: vs[:, a * 128 : b * 128],
            None,
        )
        mixed = dot_t(attended, ws_ref[:, 3 * WIDE :])
        first = (lat_ref[f, rows, :].astype(jnp.float32) + mixed).astype(jnp.bfloat16)
        firsts[f, rows, :] = first
        result = normalize(first).astype(jnp.bfloat16)

        @pl.when(k < last)
        def _():
            outgoing[f, k] = result
            send_plane(f, k).start()

        @pl.when(k == last)
        def _():
            hall[1, frames * sub + f] = result
            pass_on(f, last)

        @pl.when(k > 0)
        def _():
            send_plane(f, k - 1).wait_recv()
            pass_on(f, k - 1)

        return carry

    lax.fori_loop(0, frames * PLANE, step, 0)

    time = PLANE * frames
    row = lax.broadcasted_iota(jnp.int32, bias.shape, 0)
    col = lax.broadcasted_iota(jnp.int32, bias.shape, 1)
    mine = row // CLUSTER
    begin = mine // frames * frames - (WIN // 2 - 1)
    for i in range(PLANE):
        begin = begin + jnp.where(mine // frames == i, off_ref[i], 0)
    side = col // (CLUSTER * time) - 1
    other = col // CLUSTER - time
    valid = (
        (lax.rem(row, CLUSTER) == lax.rem(col, CLUSTER))
        & (other >= begin) & (other < begin + WIN)
        & (level + side >= 0) & (level + side < levels)
    )
    bias[...] = jnp.where(valid, 0.0, -1e30)

    def project(at):
        flat = hall[at].reshape(time * spots, C)
        low = 0 if at == 1 else WIDE
        result = dot(flat, wt_ref[:, low : 3 * WIDE]).astype(jnp.bfloat16)
        tproj[at, :, :, low:] = result.reshape(time, spots, 3 * WIDE - low)

    project(1)

    for f in range(frames):
        for k in range(PLANE):
            @pl.when(has_down)
            def _():
                send_level(f, k, True).wait_recv()

            @pl.when(has_up)
            def _():
                send_level(f, k, False).wait_recv()

    project(0)
    project(2)

    piece = spots // PIECES

    def send_back(c, k):
        to = lax.rem(sub + 1 + k, PLANE)
        rows = pl.ds(pl.multiple_of(c * piece, 16), piece)
        return remote(
            tatt.at[pl.ds(frames * to, frames), rows], back.at[sub, :, rows],
            bsend.at[c, k], brecv.at[c, k], base + to,
        )

    def temporal(c, carry):
        for inner in range(piece // CLUSTER):
            at = pl.multiple_of(c * piece + inner * CLUSTER, CLUSTER)
            spot = pl.ds(at, CLUSTER)

            def near(low):
                def get(a, b):
                    got = tproj[:, :, spot, low + a * 128 : low + b * 128]
                    return got.reshape(3 * time * CLUSTER, (b - a) * 128)
                return get

            attended = heads_of(
                lambda a, b: tproj[1, :, spot, a * 128 : b * 128].reshape(
                    time * CLUSTER, (b - a) * 128
                ),
                near(WIDE), near(2 * WIDE), bias[...],
            )
            tatt[:, spot, :] = attended.reshape(time, CLUSTER, WIDE)
        for k in range(last):
            send_back(c, k).start()
        return carry

    lax.fori_loop(0, PIECES, temporal, 0)

    def finish(which, values):
        rows = pl.ds(pl.multiple_of(which * spots, 16), spots)
        for f in range(frames):
            second = dot_t(values(f), wt_ref[:, 3 * WIDE :])
            out_ref[f, rows, :] = (firsts[f, rows, :].astype(jnp.float32) + second).astype(
                jnp.bfloat16
            )

    finish(sub, lambda f: tatt[frames * sub + f])
    for k in range(last):
        for c in range(PIECES):
            send_back(c, k).wait_recv()
        source = lax.rem(sub + PLANE - 1 - k, PLANE)
        finish(source, lambda f: back[source, f])
    for k in range(last):
        for c in range(PIECES):
            send_back(c, k).wait_send()
        for f in range(frames):
            send_plane(f, k).wait_send()
    for f in range(frames):
        for k in range(PLANE):
            @pl.when(has_up)
            def _():
                send_level(f, k, True).wait_send()

            @pl.when(has_down)
            def _():
                send_level(f, k, False).wait_send()


def block(latents, ws, picked, wt, offs, n, ident):
    frames = latents.shape[0]
    spots = HW // PLANE
    time = PLANE * frames
    vmem = pl.BlockSpec(memory_space=pltpu.VMEM)
    dma = pltpu.SemaphoreType.DMA
    bf = jnp.bfloat16
    return pl.pallas_call(
        functools.partial(block_kernel, n),
        out_shape=jax.ShapeDtypeStruct(latents.shape, bf),
        in_specs=[vmem] * 4 + [pl.BlockSpec(memory_space=pltpu.SMEM)],
        out_specs=vmem,
        scratch_shapes=[
            pltpu.VMEM((HW, WIDE), bf),
            pltpu.VMEM((2 * HW, WIDE), bf),
            pltpu.VMEM((2 * HW, WIDE), bf),
            pltpu.VMEM((frames, HW, C), bf),
            pltpu.VMEM((frames, PLANE - 1, spots, C), bf),
            pltpu.VMEM((3, time, spots, C), bf),
            pltpu.VMEM((3, time, spots, 3 * WIDE), bf),
            pltpu.VMEM((time * CLUSTER, 3 * time * CLUSTER), jnp.float32),
            pltpu.VMEM((time, spots, WIDE), bf),
            pltpu.VMEM((PLANE, frames, spots, WIDE), bf),
            dma((frames, PLANE)), dma((frames, PLANE)),
            dma((2, frames, PLANE)), dma((2, frames, PLANE)),
            dma((PIECES, PLANE)), dma((PIECES, PLANE)),
        ],
        compiler_params=pltpu.CompilerParams(
            collective_id=ident, has_side_effects=True, vmem_limit_bytes=VMEM_LIMIT
        ),
    )(latents, ws, picked, wt, offs)


def widen(weights):
    parts = weights.reshape(weights.shape[0], 4, INNER)
    parts = jnp.pad(parts, ((0, 0), (0, 0), (0, WIDE - INNER)))
    return parts.reshape(weights.shape[0], 4 * WIDE)


def body(
    latents, offsets, source_device, reference_bank,
    spatial_in, spatial_out, temporal_in, temporal_out,
):
    n = lax.axis_size("frame")
    depth = spatial_in.shape[0]
    held = up16(depth + 1)

    packed_t = widen(jnp.concatenate([temporal_in, temporal_out.T], axis=1))
    wt = lax.all_gather(packed_t, "frame", axis=0, tiled=True)

    packed_s = widen(jnp.concatenate([spatial_in, spatial_out.T], axis=1))
    mark = jnp.broadcast_to(offsets.astype(jnp.bfloat16)[:, None], (1, 4 * WIDE))
    packed_s = jnp.concatenate(
        [packed_s, mark, jnp.zeros((held - depth - 1, 4 * WIDE), jnp.bfloat16)], axis=0
    )
    picked, gathered = collect(source_device, reference_bank, packed_s, n, 0)
    ws = gathered[:, :depth].reshape(C, 4 * WIDE)
    level = lax.axis_index("frame") // PLANE
    offs = lax.dynamic_slice_in_dim(gathered[:, depth, 0], level * PLANE, PLANE, 0)
    return block(latents, ws, picked.reshape(HW, C), wt, offs.astype(jnp.int32), n, 1)


def solution(mesh):
    placed = (
        P(("clip", "frame"), None, None),
        P(("clip", "frame")),
        P("clip"),
        P(("clip", "frame"), None, None),
        P("frame", None),
        P(None, "frame"),
        P("frame", None),
        P(None, "frame"),
    )
    return jax.shard_map(
        body, mesh=mesh, in_specs=placed,
        out_specs=P(("clip", "frame"), None, None), check_vma=False,
    )
```

```python
import functools
import math

import jax
import jax.numpy as jnp
from jax import lax
from jax.experimental import pallas as pl
from jax.experimental.pallas import tpu as pltpu
from jax.sharding import PartitionSpec as P

C = 640
HW = 576
HEADS = 4
HEAD_DIM = 80
INNER = 320
WIDE = 384
WIN = 16
PLANE = 4
CLUSTER = 16
PIECES = 3
MESH = pl.DeviceIdType.MESH
FACTOR = HEAD_DIM ** (-0.5) * math.log2(math.e)
VMEM_LIMIT = 60 * 1024 * 1024
SPANS = tuple(
    (h * HEAD_DIM // 128, (h * HEAD_DIM + HEAD_DIM - 1) // 128 + 1) for h in range(HEADS)
)


def up16(count):
    return -(-count // 16) * 16


def normalize(values):
    values = values.astype(jnp.float32)
    center = values - jnp.mean(values, axis=-1, keepdims=True)
    spread = jnp.mean(center * center, axis=-1, keepdims=True)
    return center * lax.rsqrt(spread + 1e-05)


def dot(a, b):
    return jnp.dot(a, b, preferred_element_type=jnp.float32)


def dot_t(a, b):
    return lax.dot_general(a, b, (((1,), (1,)), ((), ())), preferred_element_type=jnp.float32)


def remote(src, dst, send, recv, peer):
    return pltpu.make_async_remote_copy(
        src_ref=src, dst_ref=dst, send_sem=send, recv_sem=recv,
        device_id={"frame": peer}, device_id_type=MESH,
    )


def same_chip(me):
    return me + 1 - 2 * lax.rem(me, 2)


def across(me):
    return me // PLANE * PLANE + lax.rem(lax.rem(me, PLANE) + 2, PLANE)


class Relay:
    def __init__(self, n, wall, send, recv):
        self.n, self.levels = n, n // PLANE
        self.wall, self.send, self.recv = wall, send, recv
        self.me = lax.axis_index("frame")
        self.mates = (None, across(self.me), same_chip(self.me))

    def along(self, k):
        part = self.wall.at[self.me]
        return remote(
            part, part, self.send.at[0, k], self.recv.at[0, k],
            lax.rem(self.me + PLANE * k, self.n),
        )

    def hop(self, stage, origin, k, slot):
        part = self.wall.at[lax.rem(origin + self.n - PLANE * k, self.n)]
        return remote(
            part, part, self.send.at[stage, slot], self.recv.at[stage, slot], self.mates[stage]
        )

    def begin(self):
        for k in range(1, self.levels):
            self.along(k).start()
        self.hop(1, self.me, 0, 0).start()
        self.hop(2, self.me, 0, 0).start()

    def second(self):
        for k in range(1, self.levels):
            self.along(k).wait_recv()
            self.hop(1, self.me, k, k).start()
            self.hop(2, self.me, k, k).start()

    def third(self):
        for k in range(self.levels):
            self.hop(1, self.mates[1], k, k).wait_recv()
            self.hop(2, self.mates[1], k, self.levels + k).start()

    def arrive(self):
        for k in range(self.levels):
            self.hop(2, self.mates[2], k, k).wait_recv()
            self.hop(2, across(self.mates[2]), k, self.levels + k).wait_recv()

    def drain(self):
        for k in range(self.levels):
            if k:
                self.along(k).wait_send()
            self.hop(1, self.me, k, k).wait_send()
            self.hop(2, self.me, k, k).wait_send()
            self.hop(2, self.mates[1], k, self.levels + k).wait_send()


def collect_kernel(
    n, rows, holders, src_ref, bank_ref, w_ref, ref_ref, wall_ref,
    pair, cross, out_x, out_z, got, chunk, csend, crecv, zsend, zrecv, wsend, wrecv, local,
):
    me = lax.axis_index("frame")
    sub, level = lax.rem(me, PLANE), me // PLANE
    levels = n // PLANE
    xmate, cmate = across(me), same_chip(me)
    spots = HW // PLANE
    core, side = lax.rem(me, 2), lax.rem(me, PLANE) // 2
    barrier = pltpu.get_barrier_semaphore()
    peers = [xmate, cmate] + [lax.rem(me + PLANE * k, n) for k in range(1, levels)]
    for peer in peers:
        pl.semaphore_signal(barrier, inc=1, device_id={"frame": peer}, device_id_type=MESH)
    place = pltpu.make_async_copy(w_ref, wall_ref.at[me], local.at[0])
    place.start()

    def bank_rows(x, c):
        start = pl.multiple_of((2 * x + c) * spots, 16)
        return bank_ref.at[0, pl.ds(start, spots)]

    for x in range(2):
        pltpu.make_async_copy(bank_rows(x, core), pair.at[1, x], local.at[1 + x]).start()
    pl.semaphore_wait(barrier, len(peers))

    def core_copy(x):
        return remote(bank_rows(x, 1 - core), pair.at[0, x], csend.at[x], crecv.at[x], cmate)

    for x in range(2):
        core_copy(x).start()
    relay = Relay(n, wall_ref, wsend, wrecv)
    place.wait()
    relay.begin()
    source = src_ref[0]
    for x in range(2):
        pltpu.make_async_copy(bank_rows(x, core), pair.at[1, x], local.at[1 + x]).wait()
        core_copy(x).wait_recv()
    pick = (source == me).astype(jnp.int32)
    out_x[...] = pair[pick, 1 - side]
    x_copy = remote(out_x, cross.at[0], csend.at[2], crecv.at[2], xmate)
    x_copy.start()
    cross[1] = pair[pick, side]
    x_copy.wait_recv()
    pick = (source // 2 == me // 2).astype(jnp.int32)
    out_z[...] = cross[pick]

    def spread(k):
        peer_level = lax.rem(level + k, levels)
        start = pl.multiple_of(peer_level * rows, 16)
        return peer_level, remote(
            out_z.at[pl.ds(start, rows)], got.at[level], zsend.at[0, k], zrecv.at[0, k],
            lax.rem(me + PLANE * k, n),
        )

    for k in range(1, levels):
        @pl.when(lax.rem(level + k, levels) < holders)
        def _():
            spread(k)[1].start()

    def gather(k, origin):
        part = ref_ref.at[sub, origin]
        return remote(
            chunk, part, zsend.at[1, k], zrecv.at[1, k], lax.rem(me + PLANE * k, n)
        )

    @pl.when(level < holders)
    def _():
        got[level] = out_z[pl.ds(pl.multiple_of(level * rows, 16), rows), :]
        for k in range(1, levels):
            remote(
                out_z.at[pl.ds(0, rows)], got.at[lax.rem(level + levels - k, levels)],
                zsend.at[0, k], zrecv.at[0, k], lax.rem(me + PLANE * k, n),
            ).wait_recv()
        chunk[...] = got[source // PLANE]
        for k in range(1, levels):
            gather(k, level).start()
        own = pltpu.make_async_copy(chunk, ref_ref.at[sub, level], local.at[1])
        own.start()
        own.wait()

    relay.second()
    for k in range(1, levels):
        sender = lax.rem(level + levels - k, levels)

        @pl.when(sender < holders)
        def _():
            gather(k, sender).wait_recv()

    other = lax.rem(sub + 2, PLANE)

    def plane_copy(which, slot, peer):
        return remote(
            ref_ref.at[which], ref_ref.at[which], csend.at[slot], crecv.at[slot], peer
        )

    plane_copy(sub, 3, xmate).start()
    plane_copy(sub, 4, cmate).start()
    relay.third()
    plane_copy(other, 3, xmate).wait_recv()
    plane_copy(other, 5, cmate).start()
    relay.arrive()
    plane_copy(lax.rem(cmate, PLANE), 4, cmate).wait_recv()
    plane_copy(lax.rem(across(cmate), PLANE), 5, cmate).wait_recv()
    relay.drain()
    for x in range(2):
        core_copy(x).wait_send()
    x_copy.wait_send()
    plane_copy(sub, 3, xmate).wait_send()
    plane_copy(sub, 4, cmate).wait_send()
    plane_copy(other, 5, cmate).wait_send()
    for k in range(1, levels):
        @pl.when(lax.rem(level + k, levels) < holders)
        def _():
            spread(k)[1].wait_send()

        @pl.when(level < holders)
        def _():
            gather(k, level).wait_send()


def collect(source, bank, weights, n, ident):
    spots, levels = HW // PLANE, n // PLANE
    rows = up16(-(-spots // levels))
    holders = spots // rows
    any_spec = pl.BlockSpec(memory_space=pl.ANY)
    dma = pltpu.SemaphoreType.DMA
    bf = jnp.bfloat16
    return pl.pallas_call(
        functools.partial(collect_kernel, n, rows, holders),
        out_shape=(
            jax.ShapeDtypeStruct((PLANE, holders, rows, C), bf),
            jax.ShapeDtypeStruct((n,) + weights.shape, bf),
        ),
        in_specs=[pl.BlockSpec(memory_space=pltpu.SMEM), any_spec, any_spec],
        out_specs=(any_spec, any_spec),
        scratch_shapes=[
            pltpu.VMEM((2, 2, spots, C), bf),
            pltpu.VMEM((2, spots, C), bf),
            pltpu.VMEM((spots, C), bf),
            pltpu.VMEM((spots, C), bf),
            pltpu.VMEM((levels, rows, C), bf),
            pltpu.VMEM((rows, C), bf),
            dma((6,)), dma((6,)),
            dma((2, levels)), dma((2, levels)),
            dma((3, n)), dma((3, n)),
            dma((3,)),
        ],
        compiler_params=pltpu.CompilerParams(collective_id=ident, has_side_effects=True),
    )(source, bank, weights)


def heads_of(queries, keys, values, bias):
    lane = lax.broadcasted_iota(jnp.int32, (1, WIDE), 1)
    blocks = [None] * (WIDE // 128)
    for head, (low, high) in enumerate(SPANS):
        inside = (lane >= head * HEAD_DIM) & (lane < (head + 1) * HEAD_DIM)
        inside = inside[:, low * 128 : high * 128]
        q = queries(low, high)
        q = jnp.where(inside, q, jnp.zeros_like(q))
        raw = dot_t(q, keys(low, high))
        if bias is not None:
            raw = raw + bias
        expo = jnp.exp2((raw - jnp.max(raw, axis=-1, keepdims=True)) * FACTOR)
        total = jnp.sum(expo, axis=-1, keepdims=True)
        weights = (expo * (1.0 / total)).astype(jnp.bfloat16)
        part = jnp.where(inside, dot(weights, values(low, high)), 0.0)
        for b in range(low, high):
            piece = part[:, (b - low) * 128 : (b - low + 1) * 128]
            blocks[b] = piece if blocks[b] is None else blocks[b] + piece
    return jnp.concatenate(blocks, axis=1).astype(jnp.bfloat16)


def block_kernel(
    n, depth, lat_ref, sall_ref, picked_ref, part_ref, off_ref, out_ref,
    ws_ref, wt_ref, tall, qs, ks, vs, firsts, outgoing, hall, tproj, bias, tatt, back,
    psend, precv, zsend, zrecv, bsend, brecv, wsend, wrecv,
):
    me = lax.axis_index("frame")
    levels = n // PLANE
    level, sub = me // PLANE, lax.rem(me, PLANE)
    base = level * PLANE
    frames = lat_ref.shape[0]
    spots = HW // PLANE
    barrier = pltpu.get_barrier_semaphore()
    has_down, has_up = level > 0, level < levels - 1

    def signal(peer):
        pl.semaphore_signal(barrier, inc=1, device_id={"frame": peer}, device_id_type=MESH)

    def mate(k):
        return base + lax.rem(sub + 1 + k, PLANE)

    for k in range(PLANE - 1):
        signal(mate(k))

    for k in range(1, levels):
        signal(lax.rem(me + PLANE * k, n))
    tall[me] = part_ref[...]
    pl.semaphore_wait(barrier, PLANE - 1 + levels - 1)
    relay = Relay(n, tall, wsend, wrecv)
    relay.begin()
    for i in range(n):
        ws_ref[i * depth : (i + 1) * depth, :] = sall_ref[i, :depth, :]

    @pl.when(level == 0)
    def _():
        hall[0] = jnp.zeros(hall.shape[1:], jnp.bfloat16)

    @pl.when(level == levels - 1)
    def _():
        hall[2] = jnp.zeros(hall.shape[1:], jnp.bfloat16)

    def send_plane(f, k):
        return remote(
            outgoing.at[f, k], hall.at[1, frames * sub + f],
            psend.at[f, k], precv.at[f, k], base + lax.rem(sub + 1 + k, PLANE),
        )

    def arrived(f, k):
        source = lax.rem(sub + 2 * PLANE - 1 - k, PLANE)
        return frames * source + f

    def send_level(f, k, up):
        at = arrived(f, k)
        side = 0 if up else 1
        return remote(
            hall.at[1, at], hall.at[0 if up else 2, at],
            zsend.at[side, f, k], zrecv.at[side, f, k], me + PLANE if up else me - PLANE,
        )

    def pass_on(f, k):
        @pl.when(has_up)
        def _():
            send_level(f, k, True).start()

        @pl.when(has_down)
        def _():
            send_level(f, k, False).start()

    hidden = normalize(picked_ref[...]).astype(jnp.bfloat16)
    ks[HW:, :] = dot(hidden, ws_ref[:, WIDE : 2 * WIDE]).astype(jnp.bfloat16)
    vs[HW:, :] = dot(hidden, ws_ref[:, 2 * WIDE : 3 * WIDE]).astype(jnp.bfloat16)
    last = PLANE - 1

    def step(t, carry):
        f, k = t // PLANE, lax.rem(t, PLANE)

        @pl.when(k == 0)
        def _():
            hidden = normalize(lat_ref[f]).astype(jnp.bfloat16)
            qs[...] = dot(hidden, ws_ref[:, :WIDE]).astype(jnp.bfloat16)
            ks[:HW, :] = dot(hidden, ws_ref[:, WIDE : 2 * WIDE]).astype(jnp.bfloat16)
            vs[:HW, :] = dot(hidden, ws_ref[:, 2 * WIDE : 3 * WIDE]).astype(jnp.bfloat16)

        to = lax.rem(sub + 1 + k, PLANE)
        rows = pl.ds(pl.multiple_of(to * spots, 16), spots)
        attended = heads_of(
            lambda a, b: qs[rows, a * 128 : b * 128],
            lambda a, b: ks[:, a * 128 : b * 128],
            lambda a, b: vs[:, a * 128 : b * 128],
            None,
        )
        mixed = dot_t(attended, ws_ref[:, 3 * WIDE :])
        first = (lat_ref[f, rows, :].astype(jnp.float32) + mixed).astype(jnp.bfloat16)
        firsts[f, rows, :] = first
        result = normalize(first).astype(jnp.bfloat16)

        @pl.when(k < last)
        def _():
            outgoing[f, k] = result
            send_plane(f, k).start()

        @pl.when(k == last)
        def _():
            hall[1, frames * sub + f] = result
            pass_on(f, last)

        @pl.when(k > 0)
        def _():
            send_plane(f, k - 1).wait_recv()
            pass_on(f, k - 1)

        @pl.when(t == 2)
        def _():
            relay.second()

        @pl.when(t == 5)
        def _():
            relay.third()

        return carry

    lax.fori_loop(0, frames * PLANE, step, 0)

    relay.arrive()
    for i in range(n):
        wt_ref[i * depth : (i + 1) * depth, :] = tall[i, :depth, :]
    time = PLANE * frames
    row = lax.broadcasted_iota(jnp.int32, bias.shape, 0)
    col = lax.broadcasted_iota(jnp.int32, bias.shape, 1)
    mine = row // CLUSTER
    begin = mine // frames * frames - (WIN // 2 - 1)
    for i in range(PLANE):
        begin = begin + jnp.where(mine // frames == i, off_ref[i], 0)
    side = col // (CLUSTER * time) - 1
    other = col // CLUSTER - time
    valid = (
        (lax.rem(row, CLUSTER) == lax.rem(col, CLUSTER))
        & (other >= begin) & (other < begin + WIN)
        & (level + side >= 0) & (level + side < levels)
    )
    bias[...] = jnp.where(valid, 0.0, -1e30)

    def project(at):
        flat = hall[at].reshape(time * spots, C)
        low = 0 if at == 1 else WIDE
        result = dot(flat, wt_ref[:, low : 3 * WIDE]).astype(jnp.bfloat16)
        tproj[at, :, :, low:] = result.reshape(time, spots, 3 * WIDE - low)

    project(1)

    for f in range(frames):
        for k in range(PLANE):
            @pl.when(has_down)
            def _():
                send_level(f, k, True).wait_recv()

            @pl.when(has_up)
            def _():
                send_level(f, k, False).wait_recv()

    project(0)
    project(2)

    piece = spots // PIECES

    def send_back(c, k):
        to = lax.rem(sub + 1 + k, PLANE)
        rows = pl.ds(pl.multiple_of(c * piece, 16), piece)
        return remote(
            tatt.at[pl.ds(frames * to, frames), rows], back.at[sub, :, rows],
            bsend.at[c, k], brecv.at[c, k], base + to,
        )

    def temporal(c, carry):
        for inner in range(piece // CLUSTER):
            at = pl.multiple_of(c * piece + inner * CLUSTER, CLUSTER)
            spot = pl.ds(at, CLUSTER)

            def near(low):
                def get(a, b):
                    got = tproj[:, :, spot, low + a * 128 : low + b * 128]
                    return got.reshape(3 * time * CLUSTER, (b - a) * 128)
                return get

            attended = heads_of(
                lambda a, b: tproj[1, :, spot, a * 128 : b * 128].reshape(
                    time * CLUSTER, (b - a) * 128
                ),
                near(WIDE), near(2 * WIDE), bias[...],
            )
            tatt[:, spot, :] = attended.reshape(time, CLUSTER, WIDE)
        for k in range(last):
            send_back(c, k).start()
        return carry

    lax.fori_loop(0, PIECES, temporal, 0)

    def finish(which, values):
        rows = pl.ds(pl.multiple_of(which * spots, 16), spots)
        for f in range(frames):
            second = dot_t(values(f), wt_ref[:, 3 * WIDE :])
            out_ref[f, rows, :] = (firsts[f, rows, :].astype(jnp.float32) + second).astype(
                jnp.bfloat16
            )

    finish(sub, lambda f: tatt[frames * sub + f])
    for k in range(last):
        for c in range(PIECES):
            send_back(c, k).wait_recv()
        source = lax.rem(sub + PLANE - 1 - k, PLANE)
        finish(source, lambda f: back[source, f])
    relay.drain()
    for k in range(last):
        for c in range(PIECES):
            send_back(c, k).wait_send()
        for f in range(frames):
            send_plane(f, k).wait_send()
    for f in range(frames):
        for k in range(PLANE):
            @pl.when(has_up)
            def _():
                send_level(f, k, True).wait_send()

            @pl.when(has_down)
            def _():
                send_level(f, k, False).wait_send()


def block(latents, sall, picked, part, offs, depth, n, ident):
    frames = latents.shape[0]
    spots = HW // PLANE
    time = PLANE * frames
    vmem = pl.BlockSpec(memory_space=pltpu.VMEM)
    dma = pltpu.SemaphoreType.DMA
    bf = jnp.bfloat16
    return pl.pallas_call(
        functools.partial(block_kernel, n, depth),
        out_shape=jax.ShapeDtypeStruct(latents.shape, bf),
        in_specs=[vmem] * 4 + [pl.BlockSpec(memory_space=pltpu.SMEM)],
        out_specs=vmem,
        scratch_shapes=[
            pltpu.VMEM((C, 4 * WIDE), bf),
            pltpu.VMEM((C, 4 * WIDE), bf),
            pltpu.VMEM((n,) + part.shape, bf),
            pltpu.VMEM((HW, WIDE), bf),
            pltpu.VMEM((2 * HW, WIDE), bf),
            pltpu.VMEM((2 * HW, WIDE), bf),
            pltpu.VMEM((frames, HW, C), bf),
            pltpu.VMEM((frames, PLANE - 1, spots, C), bf),
            pltpu.VMEM((3, time, spots, C), bf),
            pltpu.VMEM((3, time, spots, 3 * WIDE), bf),
            pltpu.VMEM((time * CLUSTER, 3 * time * CLUSTER), jnp.float32),
            pltpu.VMEM((time, spots, WIDE), bf),
            pltpu.VMEM((PLANE, frames, spots, WIDE), bf),
            dma((frames, PLANE)), dma((frames, PLANE)),
            dma((2, frames, PLANE)), dma((2, frames, PLANE)),
            dma((PIECES, PLANE)), dma((PIECES, PLANE)),
            dma((3, n)), dma((3, n)),
        ],
        compiler_params=pltpu.CompilerParams(
            collective_id=ident, has_side_effects=True, vmem_limit_bytes=VMEM_LIMIT
        ),
    )(latents, sall, picked, part, offs)


def widen(weights):
    parts = weights.reshape(weights.shape[0], 4, INNER)
    parts = jnp.pad(parts, ((0, 0), (0, 0), (0, WIDE - INNER)))
    return parts.reshape(weights.shape[0], 4 * WIDE)


def body(
    latents, offsets, source_device, reference_bank,
    spatial_in, spatial_out, temporal_in, temporal_out,
):
    n = lax.axis_size("frame")
    depth = spatial_in.shape[0]
    held = up16(depth + 1)

    packed_t = widen(jnp.concatenate([temporal_in, temporal_out.T], axis=1))
    packed_t = jnp.pad(packed_t, ((0, up16(depth) - depth), (0, 0)))

    packed_s = widen(jnp.concatenate([spatial_in, spatial_out.T], axis=1))
    mark = jnp.broadcast_to(offsets.astype(jnp.bfloat16)[:, None], (1, 4 * WIDE))
    packed_s = jnp.concatenate(
        [packed_s, mark, jnp.zeros((held - depth - 1, 4 * WIDE), jnp.bfloat16)], axis=0
    )
    picked, gathered = collect(source_device, reference_bank, packed_s, n, 0)
    level = lax.axis_index("frame") // PLANE
    offs = lax.dynamic_slice_in_dim(gathered[:, depth, 0], level * PLANE, PLANE, 0)
    picked = picked.reshape(HW, C)
    return block(latents, gathered, picked, packed_t, offs.astype(jnp.int32), depth, n, 1)


def solution(mesh):
    placed = (
        P(("clip", "frame"), None, None),
        P(("clip", "frame")),
        P("clip"),
        P(("clip", "frame"), None, None),
        P("frame", None),
        P(None, "frame"),
        P("frame", None),
        P(None, "frame"),
    )
    return jax.shard_map(
        body, mesh=mesh, in_specs=placed,
        out_specs=P(("clip", "frame"), None, None), check_vma=False,
    )
```

```python
import functools
import math

import jax
import jax.numpy as jnp
from jax import lax
from jax.experimental import pallas as pl
from jax.experimental.pallas import tpu as pltpu
from jax.sharding import PartitionSpec as P

C = 640
HW = 576
HEADS = 4
HEAD_DIM = 80
INNER = 320
WIDE = 384
WIN = 16
PLANE = 4
CLUSTER = 16
PIECES = 3
MESH = pl.DeviceIdType.MESH
FACTOR = HEAD_DIM ** (-0.5) * math.log2(math.e)
VMEM_LIMIT = 60 * 1024 * 1024
SPANS = tuple(
    (h * HEAD_DIM // 128, (h * HEAD_DIM + HEAD_DIM - 1) // 128 + 1) for h in range(HEADS)
)


def up16(count):
    return -(-count // 16) * 16


def normalize(values):
    values = values.astype(jnp.float32)
    center = values - jnp.mean(values, axis=-1, keepdims=True)
    spread = jnp.mean(center * center, axis=-1, keepdims=True)
    return center * lax.rsqrt(spread + 1e-05)


def dot(a, b):
    return jnp.dot(a, b, preferred_element_type=jnp.float32)


def dot_t(a, b):
    return lax.dot_general(a, b, (((1,), (1,)), ((), ())), preferred_element_type=jnp.float32)


def remote(src, dst, send, recv, peer):
    return pltpu.make_async_remote_copy(
        src_ref=src, dst_ref=dst, send_sem=send, recv_sem=recv,
        device_id={"frame": peer}, device_id_type=MESH,
    )


def same_chip(me):
    return me + 1 - 2 * lax.rem(me, 2)


def across(me):
    return me // PLANE * PLANE + lax.rem(lax.rem(me, PLANE) + 2, PLANE)


class Relay:
    def __init__(self, n, wall, send, recv, along=True):
        self.first = 1 if along else n
        self.n, self.levels = n, n // PLANE
        self.wall, self.send, self.recv = wall, send, recv
        self.me = lax.axis_index("frame")
        self.mates = (None, across(self.me), same_chip(self.me))

    def along(self, k):
        part = self.wall.at[self.me]
        return remote(
            part, part, self.send.at[0, k], self.recv.at[0, k],
            lax.rem(self.me + PLANE * k, self.n),
        )

    def hop(self, stage, origin, k, slot):
        part = self.wall.at[lax.rem(origin + self.n - PLANE * k, self.n)]
        return remote(
            part, part, self.send.at[stage, slot], self.recv.at[stage, slot], self.mates[stage]
        )

    def begin(self):
        for k in range(self.first, self.levels):
            self.along(k).start()
        self.hop(1, self.me, 0, 0).start()
        self.hop(2, self.me, 0, 0).start()

    def second(self):
        for k in range(1, self.levels):
            if k >= self.first:
                self.along(k).wait_recv()
            self.hop(1, self.me, k, k).start()
            self.hop(2, self.me, k, k).start()

    def third(self):
        for k in range(self.levels):
            self.hop(1, self.mates[1], k, k).wait_recv()
            self.hop(2, self.mates[1], k, self.levels + k).start()

    def arrive(self):
        for k in range(self.levels):
            self.hop(2, self.mates[2], k, k).wait_recv()
            self.hop(2, across(self.mates[2]), k, self.levels + k).wait_recv()

    def drain(self):
        for k in range(self.levels):
            if k >= self.first:
                self.along(k).wait_send()
            self.hop(1, self.me, k, k).wait_send()
            self.hop(2, self.me, k, k).wait_send()
            self.hop(2, self.mates[1], k, self.levels + k).wait_send()


def collect_kernel(
    n, rows, holders, src_ref, bank_ref, w_ref, t_ref, ref_ref, wall_ref, line_ref,
    pair, cross, out_x, out_z, got, chunk, csend, crecv, zsend, zrecv, wsend, wrecv, tsend, trecv, local,
):
    me = lax.axis_index("frame")
    sub, level = lax.rem(me, PLANE), me // PLANE
    levels = n // PLANE
    xmate, cmate = across(me), same_chip(me)
    spots = HW // PLANE
    core, side = lax.rem(me, 2), lax.rem(me, PLANE) // 2
    barrier = pltpu.get_barrier_semaphore()
    peers = [xmate, cmate] + [lax.rem(me + PLANE * k, n) for k in range(1, levels)]
    for peer in peers:
        pl.semaphore_signal(barrier, inc=1, device_id={"frame": peer}, device_id_type=MESH)
    place = pltpu.make_async_copy(w_ref, wall_ref.at[me], local.at[0])
    place.start()
    keep = pltpu.make_async_copy(t_ref, line_ref.at[level], local.at[3])
    keep.start()

    def line(k):
        return remote(
            t_ref, line_ref.at[level], tsend.at[k], trecv.at[k], lax.rem(me + PLANE * k, n)
        )

    def line_from(k):
        return remote(
            t_ref, line_ref.at[lax.rem(level + levels - k, levels)], tsend.at[k], trecv.at[k],
            lax.rem(me + PLANE * k, n),
        )

    def bank_rows(x, c):
        start = pl.multiple_of((2 * x + c) * spots, 16)
        return bank_ref.at[0, pl.ds(start, spots)]

    for x in range(2):
        pltpu.make_async_copy(bank_rows(x, core), pair.at[1, x], local.at[1 + x]).start()
    pl.semaphore_wait(barrier, len(peers))

    def core_copy(x):
        return remote(bank_rows(x, 1 - core), pair.at[0, x], csend.at[x], crecv.at[x], cmate)

    for x in range(2):
        core_copy(x).start()
    relay = Relay(n, wall_ref, wsend, wrecv)
    place.wait()
    relay.begin()
    source = src_ref[0]
    for x in range(2):
        pltpu.make_async_copy(bank_rows(x, core), pair.at[1, x], local.at[1 + x]).wait()
        core_copy(x).wait_recv()
    pick = (source == me).astype(jnp.int32)
    out_x[...] = pair[pick, 1 - side]
    x_copy = remote(out_x, cross.at[0], csend.at[2], crecv.at[2], xmate)
    x_copy.start()
    cross[1] = pair[pick, side]
    x_copy.wait_recv()
    pick = (source // 2 == me // 2).astype(jnp.int32)
    out_z[...] = cross[pick]

    def spread(k):
        peer_level = lax.rem(level + k, levels)
        start = pl.multiple_of(peer_level * rows, 16)
        return peer_level, remote(
            out_z.at[pl.ds(start, rows)], got.at[level], zsend.at[0, k], zrecv.at[0, k],
            lax.rem(me + PLANE * k, n),
        )

    for k in range(1, levels):
        @pl.when(lax.rem(level + k, levels) < holders)
        def _():
            spread(k)[1].start()

    def gather(k, origin):
        part = ref_ref.at[sub, origin]
        return remote(
            chunk, part, zsend.at[1, k], zrecv.at[1, k], lax.rem(me + PLANE * k, n)
        )

    @pl.when(level < holders)
    def _():
        got[level] = out_z[pl.ds(pl.multiple_of(level * rows, 16), rows), :]
        for k in range(1, levels):
            remote(
                out_z.at[pl.ds(0, rows)], got.at[lax.rem(level + levels - k, levels)],
                zsend.at[0, k], zrecv.at[0, k], lax.rem(me + PLANE * k, n),
            ).wait_recv()
        chunk[...] = got[source // PLANE]
        for k in range(1, levels):
            gather(k, level).start()
        own = pltpu.make_async_copy(chunk, ref_ref.at[sub, level], local.at[1])
        own.start()
        own.wait()

    relay.second()
    for k in range(1, levels):
        sender = lax.rem(level + levels - k, levels)

        @pl.when(sender < holders)
        def _():
            gather(k, sender).wait_recv()

    for k in range(1, levels):
        line(k).start()
    other = lax.rem(sub + 2, PLANE)

    def plane_copy(which, slot, peer):
        return remote(
            ref_ref.at[which], ref_ref.at[which], csend.at[slot], crecv.at[slot], peer
        )

    plane_copy(sub, 3, xmate).start()
    plane_copy(sub, 4, cmate).start()
    relay.third()
    plane_copy(other, 3, xmate).wait_recv()
    plane_copy(other, 5, cmate).start()
    relay.arrive()
    plane_copy(lax.rem(cmate, PLANE), 4, cmate).wait_recv()
    plane_copy(lax.rem(across(cmate), PLANE), 5, cmate).wait_recv()
    relay.drain()
    keep.wait()
    for k in range(1, levels):
        line_from(k).wait_recv()
        line(k).wait_send()
    for x in range(2):
        core_copy(x).wait_send()
    x_copy.wait_send()
    plane_copy(sub, 3, xmate).wait_send()
    plane_copy(sub, 4, cmate).wait_send()
    plane_copy(other, 5, cmate).wait_send()
    for k in range(1, levels):
        @pl.when(lax.rem(level + k, levels) < holders)
        def _():
            spread(k)[1].wait_send()

        @pl.when(level < holders)
        def _():
            gather(k, level).wait_send()


def collect(source, bank, weights, later, n, ident):
    spots, levels = HW // PLANE, n // PLANE
    rows = up16(-(-spots // levels))
    holders = spots // rows
    any_spec = pl.BlockSpec(memory_space=pl.ANY)
    dma = pltpu.SemaphoreType.DMA
    bf = jnp.bfloat16
    return pl.pallas_call(
        functools.partial(collect_kernel, n, rows, holders),
        out_shape=(
            jax.ShapeDtypeStruct((PLANE, holders, rows, C), bf),
            jax.ShapeDtypeStruct((n,) + weights.shape, bf),
            jax.ShapeDtypeStruct((levels,) + later.shape, bf),
        ),
        in_specs=[pl.BlockSpec(memory_space=pltpu.SMEM), any_spec, any_spec, any_spec],
        out_specs=(any_spec, any_spec, any_spec),
        scratch_shapes=[
            pltpu.VMEM((2, 2, spots, C), bf),
            pltpu.VMEM((2, spots, C), bf),
            pltpu.VMEM((spots, C), bf),
            pltpu.VMEM((spots, C), bf),
            pltpu.VMEM((levels, rows, C), bf),
            pltpu.VMEM((rows, C), bf),
            dma((6,)), dma((6,)),
            dma((2, levels)), dma((2, levels)),
            dma((3, n)), dma((3, n)),
            dma((levels,)), dma((levels,)),
            dma((4,)),
        ],
        compiler_params=pltpu.CompilerParams(collective_id=ident, has_side_effects=True),
    )(source, bank, weights, later)


def heads_of(queries, keys, values, bias):
    lane = lax.broadcasted_iota(jnp.int32, (1, WIDE), 1)
    blocks = [None] * (WIDE // 128)
    for head, (low, high) in enumerate(SPANS):
        inside = (lane >= head * HEAD_DIM) & (lane < (head + 1) * HEAD_DIM)
        inside = inside[:, low * 128 : high * 128]
        q = queries(low, high)
        q = jnp.where(inside, q, jnp.zeros_like(q))
        raw = dot_t(q, keys(low, high))
        if bias is not None:
            raw = raw + bias
        expo = jnp.exp2((raw - jnp.max(raw, axis=-1, keepdims=True)) * FACTOR)
        total = jnp.sum(expo, axis=-1, keepdims=True)
        weights = (expo * (1.0 / total)).astype(jnp.bfloat16)
        part = jnp.where(inside, dot(weights, values(low, high)), 0.0)
        for b in range(low, high):
            piece = part[:, (b - low) * 128 : (b - low + 1) * 128]
            blocks[b] = piece if blocks[b] is None else blocks[b] + piece
    return jnp.concatenate(blocks, axis=1).astype(jnp.bfloat16)


def unfold(n, depth, wall, wide):
    for j in range(4):
        wide[:, j * WIDE + INNER : (j + 1) * WIDE] = jnp.zeros(
            (n * depth, WIDE - INNER), jnp.bfloat16
        )
        for i in range(n):
            wide[i * depth : (i + 1) * depth, j * WIDE : j * WIDE + INNER] = wall[
                i, :depth, j * INNER : (j + 1) * INNER
            ]


def block_kernel(
    n, depth, lat_ref, sall_ref, picked_ref, part_ref, off_ref, out_ref,
    ws_ref, wt_ref, tall, qs, ks, vs, firsts, outgoing, hall, tproj, bias, tatt, back,
    psend, precv, zsend, zrecv, bsend, brecv, wsend, wrecv,
):
    me = lax.axis_index("frame")
    levels = n // PLANE
    level, sub = me // PLANE, lax.rem(me, PLANE)
    base = level * PLANE
    frames = lat_ref.shape[0]
    spots = HW // PLANE
    barrier = pltpu.get_barrier_semaphore()
    has_down, has_up = level > 0, level < levels - 1

    def signal(peer):
        pl.semaphore_signal(barrier, inc=1, device_id={"frame": peer}, device_id_type=MESH)

    def mate(k):
        return base + lax.rem(sub + 1 + k, PLANE)

    for k in range(PLANE - 1):
        signal(mate(k))

    for k in range(1, levels):
        signal(lax.rem(me + PLANE * k, n))
    for i in range(levels):
        tall[PLANE * i + sub] = part_ref[i]
    pl.semaphore_wait(barrier, PLANE - 1 + levels - 1)
    relay = Relay(n, tall, wsend, wrecv, along=False)
    relay.begin()
    relay.second()
    unfold(n, depth, sall_ref, ws_ref)

    @pl.when(level == 0)
    def _():
        hall[0] = jnp.zeros(hall.shape[1:], jnp.bfloat16)

    @pl.when(level == levels - 1)
    def _():
        hall[2] = jnp.zeros(hall.shape[1:], jnp.bfloat16)

    def send_plane(f, k):
        return remote(
            outgoing.at[f, k], hall.at[1, frames * sub + f],
            psend.at[f, k], precv.at[f, k], base + lax.rem(sub + 1 + k, PLANE),
        )

    def arrived(f, k):
        source = lax.rem(sub + 2 * PLANE - 1 - k, PLANE)
        return frames * source + f

    def send_level(f, k, up):
        at = arrived(f, k)
        side = 0 if up else 1
        return remote(
            hall.at[1, at], hall.at[0 if up else 2, at],
            zsend.at[side, f, k], zrecv.at[side, f, k], me + PLANE if up else me - PLANE,
        )

    def pass_on(f, k):
        @pl.when(has_up)
        def _():
            send_level(f, k, True).start()

        @pl.when(has_down)
        def _():
            send_level(f, k, False).start()

    hidden = normalize(picked_ref[...]).astype(jnp.bfloat16)
    ks[HW:, :] = dot(hidden, ws_ref[:, WIDE : 2 * WIDE]).astype(jnp.bfloat16)
    vs[HW:, :] = dot(hidden, ws_ref[:, 2 * WIDE : 3 * WIDE]).astype(jnp.bfloat16)
    last = PLANE - 1

    def step(t, carry):
        f, k = t // PLANE, lax.rem(t, PLANE)

        @pl.when(k == 0)
        def _():
            hidden = normalize(lat_ref[f]).astype(jnp.bfloat16)
            qs[...] = dot(hidden, ws_ref[:, :WIDE]).astype(jnp.bfloat16)
            ks[:HW, :] = dot(hidden, ws_ref[:, WIDE : 2 * WIDE]).astype(jnp.bfloat16)
            vs[:HW, :] = dot(hidden, ws_ref[:, 2 * WIDE : 3 * WIDE]).astype(jnp.bfloat16)

        to = lax.rem(sub + 1 + k, PLANE)
        rows = pl.ds(pl.multiple_of(to * spots, 16), spots)
        attended = heads_of(
            lambda a, b: qs[rows, a * 128 : b * 128],
            lambda a, b: ks[:, a * 128 : b * 128],
            lambda a, b: vs[:, a * 128 : b * 128],
            None,
        )
        mixed = dot_t(attended, ws_ref[:, 3 * WIDE :])
        first = (lat_ref[f, rows, :].astype(jnp.float32) + mixed).astype(jnp.bfloat16)
        firsts[f, rows, :] = first
        result = normalize(first).astype(jnp.bfloat16)

        @pl.when(k < last)
        def _():
            outgoing[f, k] = result
            send_plane(f, k).start()

        @pl.when(k == last)
        def _():
            hall[1, frames * sub + f] = result
            pass_on(f, last)

        @pl.when(k > 0)
        def _():
            send_plane(f, k - 1).wait_recv()
            pass_on(f, k - 1)

        @pl.when(t == 3)
        def _():
            relay.third()

        return carry

    lax.fori_loop(0, frames * PLANE, step, 0)

    relay.arrive()
    unfold(n, depth, tall, wt_ref)
    time = PLANE * frames
    row = lax.broadcasted_iota(jnp.int32, bias.shape, 0)
    col = lax.broadcasted_iota(jnp.int32, bias.shape, 1)
    mine = row // CLUSTER
    begin = mine // frames * frames - (WIN // 2 - 1)
    for i in range(PLANE):
        begin = begin + jnp.where(mine // frames == i, off_ref[i], 0)
    side = col // (CLUSTER * time) - 1
    other = col // CLUSTER - time
    valid = (
        (lax.rem(row, CLUSTER) == lax.rem(col, CLUSTER))
        & (other >= begin) & (other < begin + WIN)
        & (level + side >= 0) & (level + side < levels)
    )
    bias[...] = jnp.where(valid, 0.0, -1e30)

    def project(at):
        flat = hall[at].reshape(time * spots, C)
        low = 0 if at == 1 else WIDE
        result = dot(flat, wt_ref[:, low : 3 * WIDE]).astype(jnp.bfloat16)
        tproj[at, :, :, low:] = result.reshape(time, spots, 3 * WIDE - low)

    project(1)

    for f in range(frames):
        for k in range(PLANE):
            @pl.when(has_down)
            def _():
                send_level(f, k, True).wait_recv()

            @pl.when(has_up)
            def _():
                send_level(f, k, False).wait_recv()

    project(0)
    project(2)

    piece = spots // PIECES

    def send_back(c, k):
        to = lax.rem(sub + 1 + k, PLANE)
        rows = pl.ds(pl.multiple_of(c * piece, 16), piece)
        return remote(
            tatt.at[pl.ds(frames * to, frames), rows], back.at[sub, :, rows],
            bsend.at[c, k], brecv.at[c, k], base + to,
        )

    def temporal(c, carry):
        for inner in range(piece // CLUSTER):
            at = pl.multiple_of(c * piece + inner * CLUSTER, CLUSTER)
            spot = pl.ds(at, CLUSTER)

            def near(low):
                def get(a, b):
                    got = tproj[:, :, spot, low + a * 128 : low + b * 128]
                    return got.reshape(3 * time * CLUSTER, (b - a) * 128)
                return get

            attended = heads_of(
                lambda a, b: tproj[1, :, spot, a * 128 : b * 128].reshape(
                    time * CLUSTER, (b - a) * 128
                ),
                near(WIDE), near(2 * WIDE), bias[...],
            )
            tatt[:, spot, :] = attended.reshape(time, CLUSTER, WIDE)
        for k in range(last):
            send_back(c, k).start()
        return carry

    lax.fori_loop(0, PIECES, temporal, 0)

    def finish(which, values):
        rows = pl.ds(pl.multiple_of(which * spots, 16), spots)
        for f in range(frames):
            second = dot_t(values(f), wt_ref[:, 3 * WIDE :])
            out_ref[f, rows, :] = (firsts[f, rows, :].astype(jnp.float32) + second).astype(
                jnp.bfloat16
            )

    finish(sub, lambda f: tatt[frames * sub + f])
    for k in range(last):
        for c in range(PIECES):
            send_back(c, k).wait_recv()
        source = lax.rem(sub + PLANE - 1 - k, PLANE)
        finish(source, lambda f: back[source, f])
    relay.drain()
    for k in range(last):
        for c in range(PIECES):
            send_back(c, k).wait_send()
        for f in range(frames):
            send_plane(f, k).wait_send()
    for f in range(frames):
        for k in range(PLANE):
            @pl.when(has_up)
            def _():
                send_level(f, k, True).wait_send()

            @pl.when(has_down)
            def _():
                send_level(f, k, False).wait_send()


def block(latents, sall, picked, part, offs, depth, n, ident):
    frames = latents.shape[0]
    spots = HW // PLANE
    time = PLANE * frames
    vmem = pl.BlockSpec(memory_space=pltpu.VMEM)
    dma = pltpu.SemaphoreType.DMA
    bf = jnp.bfloat16
    return pl.pallas_call(
        functools.partial(block_kernel, n, depth),
        out_shape=jax.ShapeDtypeStruct(latents.shape, bf),
        in_specs=[vmem] * 4 + [pl.BlockSpec(memory_space=pltpu.SMEM)],
        out_specs=vmem,
        scratch_shapes=[
            pltpu.VMEM((C, 4 * WIDE), bf),
            pltpu.VMEM((C, 4 * WIDE), bf),
            pltpu.VMEM((n,) + part.shape[1:], bf),
            pltpu.VMEM((HW, WIDE), bf),
            pltpu.VMEM((2 * HW, WIDE), bf),
            pltpu.VMEM((2 * HW, WIDE), bf),
            pltpu.VMEM((frames, HW, C), bf),
            pltpu.VMEM((frames, PLANE - 1, spots, C), bf),
            pltpu.VMEM((3, time, spots, C), bf),
            pltpu.VMEM((3, time, spots, 3 * WIDE), bf),
            pltpu.VMEM((time * CLUSTER, 3 * time * CLUSTER), jnp.float32),
            pltpu.VMEM((time, spots, WIDE), bf),
            pltpu.VMEM((PLANE, frames, spots, WIDE), bf),
            dma((frames, PLANE)), dma((frames, PLANE)),
            dma((2, frames, PLANE)), dma((2, frames, PLANE)),
            dma((PIECES, PLANE)), dma((PIECES, PLANE)),
            dma((3, n)), dma((3, n)),
        ],
        compiler_params=pltpu.CompilerParams(
            collective_id=ident, has_side_effects=True, vmem_limit_bytes=VMEM_LIMIT
        ),
    )(latents, sall, picked, part, offs)


def body(
    latents, offsets, source_device, reference_bank,
    spatial_in, spatial_out, temporal_in, temporal_out,
):
    n = lax.axis_size("frame")
    depth = spatial_in.shape[0]
    held = up16(depth + 1)

    packed_t = jnp.concatenate([temporal_in, temporal_out.T], axis=1)
    packed_t = jnp.pad(packed_t, ((0, up16(depth) - depth), (0, 0)))

    packed_s = jnp.concatenate([spatial_in, spatial_out.T], axis=1)
    mark = jnp.broadcast_to(offsets.astype(jnp.bfloat16)[:, None], (1, 4 * INNER))
    packed_s = jnp.concatenate(
        [packed_s, mark, jnp.zeros((held - depth - 1, 4 * INNER), jnp.bfloat16)], axis=0
    )
    picked, gathered, lines = collect(
        source_device, reference_bank, packed_s, packed_t, n, 0
    )
    level = lax.axis_index("frame") // PLANE
    offs = lax.dynamic_slice_in_dim(gathered[:, depth, 0], level * PLANE, PLANE, 0)
    picked = picked.reshape(HW, C)
    return block(latents, gathered, picked, lines, offs.astype(jnp.int32), depth, n, 1)


def solution(mesh):
    placed = (
        P(("clip", "frame"), None, None),
        P(("clip", "frame")),
        P("clip"),
        P(("clip", "frame"), None, None),
        P("frame", None),
        P(None, "frame"),
        P("frame", None),
        P(None, "frame"),
    )
    return jax.shard_map(
        body, mesh=mesh, in_specs=placed,
        out_specs=P(("clip", "frame"), None, None), check_vma=False,
    )
```
